768 devices in a mesh: row: 16 (over x, z_lo), col: 8 (over y), rep: 6 (over z_hi, core).
Axes of the slice: x: 4, y: 8, z: 12 (z_hi: 3, z_lo: 4; z = z_hi * 4 + z_lo), core: 2. Of those that a mesh axis runs over, the one named last changes fastest.
Arguments:
- features: bfloat16 [16, 6144, 256], P('row', ('col', 'rep')), may hold values from -6 to 6
- adj_tiles: bfloat16 [16, 48, 32, 128, 128], P('row', ('col', 'rep'))
- tile_rows: int32 [16, 48, 32], P('row', ('col', 'rep')), may hold values from 0 to 47
- tile_cols: int32 [16, 48, 32], P('row', ('col', 'rep')), may hold values from 0 to 15
- tile_count: int32 [16, 48], P('row', ('col', 'rep')), may hold values from 4 to 32, as said below
- weight: bfloat16 [256, 256], replicated, may hold values from -0.375 to 0.375
- cotangent: bfloat16 [98304, 256], P('row'), may hold values from -6 to 6
Outputs:
- layer_out: bfloat16 [98304, 256], P(('row', 'col', 'rep'))
- feature_grad: bfloat16 [16, 6144, 256], P('row', ('col', 'rep'))
The draws below stay inside these ranges and needn't reach their ends.
Inputs may be any that keep to these rules, and one draw needn't show every extreme that they name: `tile_count`: slots at or past a grid cell's count are not part of the adjacency. Each count is 32 divided by 1, 2, 4 or 8, and some grid cell holds 32.
All inputs are finite; a program needn't handle non-finite values.
Results may differ from the reference program's by a relative error of at most 0.025.
Values may be sent and summed in bfloat16 or wider, within the bound.
No kernel may reach another device: no remote copies, remote signals or barrier semaphores. Data moves between devices by JAX's collectives and lax.ppermute only.
A program may use at most 64 MiB of HBM per device.

```python
import jax
import jax.numpy as jnp
from jax import lax

F = 256
TILE = 128
TMAX = 32
NODE_DEV = 128
SECTIONS = 48
NODES = 98304
N_ROW = 16


def draw_adj_tiles(key, part):
    key = jax.random.fold_in(key, 11)
    shape = (N_ROW, SECTIONS, TMAX, TILE, TILE)
    factor = (TMAX * TILE * TILE / (2.0 * NODE_DEV)) ** (-0.5)
    values = jax.random.normal(key, shape, jnp.float32)
    return (values * factor).astype(jnp.bfloat16)


def draw_tile_count(key, part):
    key = jax.random.fold_in(key, 23)
    first, second = jax.random.split(key)
    shifts = jax.random.randint(first, (N_ROW * SECTIONS,), 0, 4)
    counts = jnp.where(shifts == 0, TMAX, jnp.where(shifts == 1, TMAX // 2, jnp.where(shifts == 2, TMAX // 4, TMAX // 8)))
    forced = jax.random.randint(second, (), 0, N_ROW * SECTIONS)
    counts = jnp.where(jnp.arange(N_ROW * SECTIONS) == forced, TMAX, counts)
    return counts.reshape(N_ROW, SECTIONS).astype(jnp.int32)


def with_ends(values, stream_key, smallest, high):
    longest = values.shape.index(max(values.shape))
    spots = []
    for shift in (0, 1):
        where = [jax.random.randint(jax.random.fold_in(stream_key, axis), (), 0, length) for axis, length in enumerate(values.shape)]
        where[longest] = (where[longest] + shift) % values.shape[longest]
        spots.append(tuple(where))
    return values.at[spots[0]].set(smallest).at[spots[1]].set(high)


def block_scale(stream_key, extent, cuts, low, high):
    def one(position, blocks):
        heights = jax.random.uniform(jax.random.fold_in(jax.random.fold_in(stream_key, 6), position), (blocks,), jnp.float32, low / len(cuts), high / len(cuts))
        return jnp.repeat(jnp.exp(heights), extent[position] // blocks).reshape((-1,) + (1,) * (len(extent) - position - 1))

    loudness = one(*cuts[0])
    for cut in cuts[1:]:
        loudness = loudness * one(*cut)
    return loudness


def scatter_about(key, extent, scale, reach, pieces=(), kind=jnp.bfloat16):
    drawn = scale * jax.random.normal(key, extent, jnp.float32)
    if pieces:
        drawn = drawn * block_scale(key, extent, pieces, -0.22, 0.18)
    return jnp.clip(drawn, -reach, reach).astype(kind)


def setup_inputs(seed: int = 0) -> dict:
    streams_of = jax.random.split(jax.random.key(seed), 8)
    return {
        "features": scatter_about(streams_of[0], (N_ROW, NODES // N_ROW, F), 1.0, 6.0, ((0, 16), (1, 48))),
        "adj_tiles": draw_adj_tiles(jax.random.fold_in(streams_of[7], 71), 0),
        "tile_rows": with_ends(jax.random.randint(streams_of[2], (N_ROW, SECTIONS, TMAX), 0, NODE_DEV * SECTIONS // TILE), jax.random.fold_in(streams_of[2], 1), 0, (NODE_DEV * SECTIONS // TILE) - 1).astype(jnp.int32),
        "tile_cols": with_ends(jax.random.randint(streams_of[3], (N_ROW, SECTIONS, TMAX), 0, NODE_DEV * N_ROW // TILE), jax.random.fold_in(streams_of[3], 1), 0, (NODE_DEV * N_ROW // TILE) - 1).astype(jnp.int32),
        "tile_count": draw_tile_count(jax.random.fold_in(streams_of[7], 71), 0),
        "weight": scatter_about(streams_of[5], (F, F), F ** -0.5, 0.375),
        "cotangent": scatter_about(streams_of[6], (NODES, F), 1.0, 6.0, ((0, 16),)),
    }


def tile_sum(tiles_wide, src_index, out_index, live_count, source, out_tiles, einsum_form):
    picked = jnp.take(source, src_index, axis=0).astype(jnp.float32)
    product = jnp.einsum(einsum_form, tiles_wide, picked, precision=lax.Precision.HIGHEST)
    slot = jnp.arange(tiles_wide.shape[0], dtype=jnp.int32)
    live_mask = slot < live_count
    target = jnp.arange(out_tiles, dtype=jnp.int32)
    onehot = ((out_index[None, :] == target[:, None]) & live_mask[None, :]).astype(jnp.float32)
    summed = jnp.einsum('rt,tif->rif', onehot, product, precision=lax.Precision.HIGHEST)
    return summed.reshape(out_tiles * tiles_wide.shape[1], -1)

def pre_grad(pre_act, cotangent):
    sigma = jax.nn.sigmoid(pre_act)
    return (cotangent.astype(jnp.float32) * sigma * (1.0 + pre_act * (1.0 - sigma))).astype(jnp.bfloat16)

def reference(features, adj_tiles, tile_rows, tile_cols, tile_count, weight, cotangent):
    feat_width = weight.shape[1]
    row_len = NODE_DEV * SECTIONS
    col_len = NODE_DEV * N_ROW
    col_blocks = features.reshape(N_ROW, SECTIONS, NODE_DEV, feat_width).transpose(1, 0, 2, 3)
    col_blocks = col_blocks.reshape(SECTIONS, col_len // TILE, TILE, feat_width)

    def forward_row(row_idx):

        def advance(carry, section):
            part = tile_sum(adj_tiles[row_idx, section].astype(jnp.float32), tile_cols[row_idx, section], tile_rows[row_idx, section], tile_count[row_idx, section], col_blocks[section], row_len // TILE, 'tij,tjf->tif')
            return (carry + part, None)
        total, _ = lax.scan(advance, jnp.zeros((row_len, feat_width), jnp.float32), jnp.arange(SECTIONS, dtype=jnp.int32))
        return total
    aggregated = lax.map(forward_row, jnp.arange(N_ROW, dtype=jnp.int32)).reshape(N_ROW * row_len, feat_width)
    pre_act = jnp.dot(aggregated.astype(jnp.bfloat16), weight, preferred_element_type=jnp.float32)
    layer_out = jax.nn.silu(pre_act).astype(jnp.bfloat16)
    grad_low = pre_grad(pre_act, cotangent)
    grad_agg = jnp.dot(grad_low, weight.T, preferred_element_type=jnp.float32).astype(jnp.bfloat16)
    grad_blocks = grad_agg.reshape(N_ROW, row_len // TILE, TILE, feat_width)

    def backward_col(section):

        def advance(carry, row_idx):
            part = tile_sum(adj_tiles[row_idx, section].astype(jnp.float32), tile_rows[row_idx, section], tile_cols[row_idx, section], tile_count[row_idx, section], grad_blocks[row_idx], col_len // TILE, 'tji,tjf->tif')
            return (carry + part, None)
        total, _ = lax.scan(advance, jnp.zeros((col_len, feat_width), jnp.float32), jnp.arange(N_ROW, dtype=jnp.int32))
        return total
    col_sums = lax.map(backward_col, jnp.arange(SECTIONS, dtype=jnp.int32)).astype(jnp.bfloat16)
    feature_grad = col_sums.reshape(SECTIONS, N_ROW, NODE_DEV, feat_width).transpose(1, 0, 2, 3)
    feature_grad = feature_grad.reshape(N_ROW, SECTIONS * NODE_DEV, feat_width)
    return (layer_out, feature_grad)
```

```python
import functools

import jax
import jax.numpy as jnp
from jax import lax
from jax.experimental import pallas as pl
from jax.experimental.pallas import tpu as pltpu
from jax.sharding import Mesh
from jax.sharding import PartitionSpec as P

TILE = 128
F = 256
X, ZL, Y, ZH, CORE = 4, 4, 8, 3, 2
ROWS = Y * ZH * CORE
COLS = X * ZL
BF = jnp.bfloat16
F32 = jnp.float32
UNROLL = 4


def forward_kernel(rows_ref, cols_ref, count_ref, adj_ref, panels_ref, out_ref, acc_ref):
    acc_ref[...] = jnp.zeros_like(acc_ref)

    def step(i, carry):
        products = []
        for k in range(UNROLL):
            t = i * UNROLL + k
            products.append(
                jnp.dot(adj_ref[t], panels_ref[cols_ref[t]], preferred_element_type=F32)
            )
        for k in range(UNROLL):
            row = rows_ref[i * UNROLL + k]
            acc_ref[row] += products[k]
        return carry

    lax.fori_loop(0, count_ref[0] // UNROLL, step, 0)

    def put(j, carry):
        for core in range(CORE):
            out_ref[core, j] = acc_ref[j * CORE + core].astype(BF)
        return carry

    lax.fori_loop(0, Y * ZH, put, 0)


def backward_kernel(rows_ref, cols_ref, count_ref, adj_ref, grads_ref, out_ref, acc_ref):
    acc_ref[...] = jnp.zeros_like(acc_ref)

    def step(i, carry):
        products = []
        for k in range(UNROLL):
            t = i * UNROLL + k
            row = rows_ref[t]
            grad = grads_ref[row % CORE, row // CORE]
            products.append(
                lax.dot_general(
                    adj_ref[t], grad, (((0,), (0,)), ((), ())), preferred_element_type=F32
                )
            )
        for k in range(UNROLL):
            acc_ref[cols_ref[i * UNROLL + k]] += products[k]
        return carry

    lax.fori_loop(0, count_ref[0] // UNROLL, step, 0)
    out_ref[...] = acc_ref[...].astype(BF)


def middle_kernel(parts_ref, weight_ref, cotangent_ref, layer_ref, grad_ref):
    summed = parts_ref[0].astype(F32)
    for k in range(1, ZH):
        summed = summed + parts_ref[k].astype(F32)
    weight = weight_ref[...]
    pre_act = jnp.dot(summed.astype(BF), weight, preferred_element_type=F32)
    sigma = jax.nn.sigmoid(pre_act)
    layer_ref[...] = (pre_act * sigma).astype(BF)
    grad_pre = (cotangent_ref[...].astype(F32) * sigma * (1.0 + pre_act * (1.0 - sigma))).astype(BF)
    grad_ref[...] = lax.dot_general(
        grad_pre, weight, (((1,), (1,)), ((), ())), preferred_element_type=F32
    ).astype(BF)


SMEM = pl.BlockSpec(memory_space=pltpu.SMEM)
VMEM = pl.BlockSpec(memory_space=pltpu.VMEM)
PARAMS = pltpu.CompilerParams(vmem_limit_bytes=40 * 2**20)


def slot_call(kernel, out_shape, acc_tiles):
    return pl.pallas_call(
        kernel,
        out_shape=jax.ShapeDtypeStruct(out_shape, BF),
        in_specs=[SMEM, SMEM, SMEM, VMEM, VMEM],
        out_specs=VMEM,
        scratch_shapes=[pltpu.VMEM((acc_tiles, TILE, F), F32)],
        compiler_params=PARAMS,
    )


def tile_exchange(x, axis):
    return lax.all_to_all(x, axis, 0, 0, tiled=True)


def gather_by_exchange(x, axis, n):
    return tile_exchange(jnp.broadcast_to(x[None], (n,) + x.shape), axis)


def tile_sum(x):
    return jnp.sum(x.astype(F32), axis=0)


def per_device(features, adj_tiles, tile_rows, tile_cols, tile_count, weight, cotangent):
    adj = adj_tiles[0, 0]
    rows = tile_rows[0, 0]
    cols = tile_cols[0, 0]
    count = tile_count[0]
    core = lax.axis_index("core")

    panels = gather_by_exchange(features[0], ("x", "zl"), COLS)
    partial = slot_call(forward_kernel, (CORE, Y * ZH, TILE, F), ROWS)(
        rows, cols, count, adj, panels
    )
    mine = lax.dynamic_index_in_dim(partial, core, 0, keepdims=False)
    theirs = lax.dynamic_index_in_dim(partial, 1 - core, 0, keepdims=False)
    got = lax.ppermute(theirs, "core", [(0, 1), (1, 0)])
    chip_sum = (mine.astype(F32) + got.astype(F32)).astype(BF)
    chip_sum = chip_sum.reshape(Y, ZH * TILE, F)
    y_sum = tile_sum(tile_exchange(chip_sum, "y")).astype(BF)
    parts = tile_exchange(y_sum.reshape(ZH, TILE, F), "zh")

    place = lax.axis_index(("y", "zh", "core"))
    own_grad = lax.dynamic_slice_in_dim(cotangent, place * TILE, TILE, 0)
    layer_out, grad_piece = pl.pallas_call(
        middle_kernel,
        out_shape=[jax.ShapeDtypeStruct((TILE, F), BF)] * 2,
        compiler_params=PARAMS,
    )(parts, weight, own_grad)

    grads = gather_by_exchange(grad_piece, "zh", ZH)
    grads = gather_by_exchange(grads.reshape(ZH * TILE, F), "y", Y)
    grads = grads.reshape(Y * ZH, TILE, F)
    grads = lax.all_gather(grads, "core", axis=0)
    column_part = slot_call(backward_kernel, (COLS, TILE, F), COLS)(
        rows, cols, count, adj, grads
    )
    grad_input = tile_sum(tile_exchange(column_part, ("x", "zl"))).astype(BF)
    return (layer_out, grad_input[None])


def solution(mesh):
    fine = Mesh(mesh.devices.reshape(X, ZL, Y, ZH, CORE), ("x", "zl", "y", "zh", "core"))
    row, sect = ("x", "zl"), ("y", "zh", "core")
    in_specs = (
        P(row, sect, None),
        P(row, sect, None, None, None),
        P(row, sect, None),
        P(row, sect, None),
        P(row, sect),
        P(),
        P(row, None),
    )
    out_specs = (P(row + sect, None), P(row, sect, None))
    return jax.shard_map(
        per_device, mesh=fine, in_specs=in_specs, out_specs=out_specs, check_vma=False
    )
```

```python
import jax
import jax.numpy as jnp
from jax import lax
from jax.experimental import pallas as pl
from jax.experimental.pallas import tpu as pltpu
from jax.sharding import Mesh
from jax.sharding import PartitionSpec as P

TILE = 128
F = 256
X, ZL, Y, ZH, CORE = 4, 4, 8, 3, 2
COLS = X * ZL
HALF = Y * ZH
BF = jnp.bfloat16
F32 = jnp.float32
UNROLL = 4
GATHER_PLACE = (0, 2, 4, 7, 5, 6, 3, 1)


def forward_kernel(dst_ref, src_ref, count_ref, adj_ref, panels_ref, mine_ref, theirs_ref, acc_ref):
    acc_ref[...] = jnp.zeros_like(acc_ref)

    def step(i, carry):
        products = []
        for k in range(UNROLL):
            t = i * UNROLL + k
            products.append(
                jnp.dot(adj_ref[t], panels_ref[src_ref[t]], preferred_element_type=F32)
            )
        for k in range(UNROLL):
            acc_ref[dst_ref[i * UNROLL + k]] += products[k]
        return carry

    lax.fori_loop(0, count_ref[0] // UNROLL, step, 0)
    theirs_ref[...] = acc_ref[HALF:].astype(BF)
    mine_ref[...] = acc_ref[:HALF].astype(BF)


def backward_kernel(dst_ref, src_ref, count_ref, adj_ref, own_ref, other_ref, out_ref, acc_ref):
    acc_ref[...] = jnp.zeros_like(acc_ref)

    def step(i, carry):
        products = []
        for k in range(UNROLL):
            t = i * UNROLL + k
            src = src_ref[t]
            place = lax.rem(src, HALF)
            grad = jnp.where(src < HALF, own_ref[place], other_ref[place])
            products.append(
                lax.dot_general(
                    adj_ref[t], grad, (((0,), (0,)), ((), ())), preferred_element_type=F32
                )
            )
        for k in range(UNROLL):
            acc_ref[dst_ref[i * UNROLL + k]] += products[k]
        return carry

    lax.fori_loop(0, count_ref[0] // UNROLL, step, 0)
    out_ref[...] = acc_ref[...].astype(BF)


def middle_kernel(parts_ref, weight_ref, cotangent_ref, layer_ref, grad_ref):
    summed = parts_ref[0].astype(F32)
    for k in range(1, ZH):
        summed = summed + parts_ref[k].astype(F32)
    weight = weight_ref[...]
    pre_act = jnp.dot(summed.astype(BF), weight, preferred_element_type=F32)
    sigma = jax.nn.sigmoid(pre_act)
    layer_ref[...] = (pre_act * sigma).astype(BF)
    grad_pre = (cotangent_ref[...].astype(F32) * sigma * (1.0 + pre_act * (1.0 - sigma))).astype(BF)
    grad = lax.dot_general(
        grad_pre, weight, (((1,), (1,)), ((), ())), preferred_element_type=F32
    ).astype(BF)
    for k in range(ZH):
        grad_ref[k] = grad


SMEM = pl.BlockSpec(memory_space=pltpu.SMEM)
VMEM = pl.BlockSpec(memory_space=pltpu.VMEM)
PARAMS = pltpu.CompilerParams(vmem_limit_bytes=40 * 2**20)


def exchange(x, axis):
    return lax.all_to_all(x, axis, 0, 0, tiled=True)


def repeat(x, n):
    return jnp.broadcast_to(x[None], (n,) + x.shape)


def tile_sum(x):
    return jnp.sum(x.astype(F32), axis=0).astype(BF)


def add_up(*terms):
    total = terms[0].astype(F32)
    for term in terms[1:]:
        total = total + term.astype(F32)
    return total.astype(BF)


def swap_cores(x):
    return lax.ppermute(x, "core", [(0, 1), (1, 0)])


def shift(x, by):
    return lax.ppermute(x, "y", [(y, (y + by) % Y) for y in range(Y)])


def mirrored_shift(x, by):
    pairs = []
    for y in range(Y):
        pairs.append((y * CORE, (y + by) % Y * CORE))
        pairs.append((y * CORE + 1, (y - by) % Y * CORE + 1))
    return lax.ppermute(x, ("y", "core"), pairs)


def per_device(features, adj_tiles, tile_rows, tile_cols, tile_count, weight, cotangent):
    adj = adj_tiles[0, 0]
    rows = tile_rows[0, 0]
    cols = tile_cols[0, 0]
    count = tile_count[0]
    core = lax.axis_index("core")
    y = lax.axis_index("y")

    row_core = rows % CORE
    row_zh = rows // CORE % ZH
    row_ahead = (rows // (CORE * ZH) - y) % Y
    foreign = (row_core != core).astype(jnp.int32)
    steps = jnp.where(row_core == 0, row_ahead, (Y - row_ahead) % Y)
    sent_place = foreign * HALF + steps * ZH + row_zh
    gather_place = jnp.zeros_like(rows)
    for k, place in enumerate(GATHER_PLACE):
        gather_place = jnp.where(row_ahead == k, place, gather_place)
    gather_place = foreign * HALF + gather_place * ZH + row_zh

    panels = exchange(repeat(features[0], ZL), "zl")
    panels = exchange(repeat(panels, X), "x").reshape(COLS, TILE, F)
    mine, theirs = pl.pallas_call(
        forward_kernel,
        out_shape=[jax.ShapeDtypeStruct((HALF, TILE, F), BF)] * 2,
        in_specs=[SMEM, SMEM, SMEM, VMEM, VMEM],
        out_specs=[VMEM, VMEM],
        scratch_shapes=[pltpu.VMEM((CORE * HALF, TILE, F), F32)],
        compiler_params=PARAMS,
    )(sent_place, cols, count, adj, panels)
    chip = add_up(mine, swap_cores(theirs)).reshape(Y, ZH, TILE, F)
    from_four = mirrored_shift(chip[4], 2)
    from_three = mirrored_shift(chip[3], 1)
    from_minus_three = mirrored_shift(chip[5], -1)
    ones = [mirrored_shift(chip[1], 1), mirrored_shift(chip[7], -1)]
    minus_two = mirrored_shift(add_up(chip[6], from_minus_three), -2)
    plus_two = mirrored_shift(add_up(chip[2], from_four, from_three), 2)
    y_sum = add_up(chip[0], *ones, minus_two, plus_two)
    parts = exchange(y_sum, "zh")

    place = lax.axis_index(("y", "zh", "core"))
    own_grad = lax.dynamic_slice_in_dim(cotangent, place * TILE, TILE, 0)
    layer_out, grad_copies = pl.pallas_call(
        middle_kernel,
        out_shape=[
            jax.ShapeDtypeStruct((TILE, F), BF),
            jax.ShapeDtypeStruct((ZH, TILE, F), BF),
        ],
        compiler_params=PARAMS,
    )(parts, weight, own_grad)

    here = exchange(grad_copies, "zh")
    minus_one, plus_one = shift(here, 1), shift(here, -1)
    minus_two, plus_two = shift(here, 2), shift(here, -2)
    four = mirrored_shift(jnp.where(core == 0, minus_two, plus_two), 2)
    minus_three, plus_three = shift(minus_two, 1), shift(plus_two, -1)
    own = jnp.concatenate(
        [here, minus_one, plus_one, minus_two, plus_two, four, minus_three, plus_three]
    )
    other = swap_cores(own)
    column_part = pl.pallas_call(
        backward_kernel,
        out_shape=jax.ShapeDtypeStruct((COLS, TILE, F), BF),
        in_specs=[SMEM, SMEM, SMEM, VMEM, VMEM, VMEM],
        out_specs=VMEM,
        scratch_shapes=[pltpu.VMEM((COLS, TILE, F), F32)],
        compiler_params=PARAMS,
    )(cols, gather_place, count, adj, own, other)
    x_sum = tile_sum(exchange(column_part.reshape(X, ZL, TILE, F), "x"))
    grad_input = tile_sum(exchange(x_sum, "zl"))
    return (layer_out, grad_input[None])


def solution(mesh):
    fine = Mesh(mesh.devices.reshape(X, ZL, Y, ZH, CORE), ("x", "zl", "y", "zh", "core"))
    row, sect = ("x", "zl"), ("y", "zh", "core")
    in_specs = (
        P(row, sect, None),
        P(row, sect, None, None, None),
        P(row, sect, None),
        P(row, sect, None),
        P(row, sect),
        P(),
        P(row, None),
    )
    out_specs = (P(row + sect, None), P(row, sect, None))
    return jax.shard_map(
        per_device, mesh=fine, in_specs=in_specs, out_specs=out_specs, check_vma=False
    )
```

```python
import jax
import jax.numpy as jnp
from jax import lax
from jax.experimental import pallas as pl
from jax.experimental.pallas import tpu as pltpu
from jax.sharding import Mesh
from jax.sharding import PartitionSpec as P

TILE = 128
F = 256
X, ZL, YH, YL, ZH, CORE = 4, 4, 4, 2, 3, 2
Y = YH * YL
COLS = X * ZL
HALF = Y * ZH
QUARTER = YH * ZH
BF = jnp.bfloat16
F32 = jnp.float32
UNROLL = 4


def pick_kernel(own_ref, cotangent_hbm, grads_ref, sems):
    copies = []
    for k in range(ZH):
        copies.append(
            pltpu.make_async_copy(
                cotangent_hbm.at[own_ref[0] + k * CORE], grads_ref.at[k], sems.at[k]
            )
        )
    for copy in copies:
        copy.start()
    for copy in copies:
        copy.wait()


def forward_kernel(
    dst_ref, src_ref, count_ref, adj_ref, panels_ref, mine_ref, theirs_ref, acc_ref
):
    acc_ref[...] = jnp.zeros_like(acc_ref)

    def step(i, carry):
        products = []
        for k in range(UNROLL):
            t = i * UNROLL + k
            products.append(
                jnp.dot(adj_ref[t], panels_ref[src_ref[t]], preferred_element_type=F32)
            )
        for k in range(UNROLL):
            acc_ref[dst_ref[i * UNROLL + k]] += products[k]
        return carry

    lax.fori_loop(0, count_ref[0] // UNROLL, step, 0)
    theirs_ref[...] = acc_ref[HALF:].astype(BF)
    mine_ref[...] = acc_ref[:HALF].astype(BF)

def backward_kernel(
    dst_ref, src_ref, count_ref, adj_ref, near_ref, far_ref, other_near_ref, other_far_ref,
    out_ref, acc_ref,
):
    acc_ref[...] = jnp.zeros_like(acc_ref)

    def step(i, carry):
        products = []
        for k in range(UNROLL):
            t = i * UNROLL + k
            src = src_ref[t]
            group = src // QUARTER
            place = src - group * QUARTER
            near = jnp.where(group < 2, near_ref[place], other_near_ref[place])
            far = jnp.where(group < 2, far_ref[place], other_far_ref[place])
            grad = jnp.where(lax.rem(group, 2) == 0, near, far)
            products.append(
                lax.dot_general(
                    adj_ref[t], grad, (((0,), (0,)), ((), ())), preferred_element_type=F32
                )
            )
        for k in range(UNROLL):
            acc_ref[dst_ref[i * UNROLL + k]] += products[k]
        return carry

    lax.fori_loop(0, count_ref[0] // UNROLL, step, 0)
    out_ref[...] = acc_ref[...].astype(BF)


def middle_kernel(zh_ref, parts_ref, weight_ref, cotangent_ref, layer_ref, grad_ref, out_ref):
    summed = parts_ref[0].astype(F32)
    for k in range(1, ZH):
        summed = summed + parts_ref[k].astype(F32)
    summed = summed.reshape(ZH * TILE, F)
    weight = weight_ref[...]
    pre_act = jnp.dot(summed.astype(BF), weight, preferred_element_type=F32)
    sigma = jax.nn.sigmoid(pre_act)
    out_ref[...] = (pre_act * sigma).reshape(ZH, TILE, F)
    layer_ref[...] = out_ref[zh_ref[0]].astype(BF)
    cotangent = cotangent_ref[...].reshape(ZH * TILE, F).astype(F32)
    grad_pre = (cotangent * sigma * (1.0 + pre_act * (1.0 - sigma))).astype(BF)
    grad = lax.dot_general(
        grad_pre, weight, (((1,), (1,)), ((), ())), preferred_element_type=F32
    ).astype(BF)
    grad_ref[...] = grad.reshape(ZH, TILE, F)


SMEM = pl.BlockSpec(memory_space=pltpu.SMEM)
VMEM = pl.BlockSpec(memory_space=pltpu.VMEM)
HBM = pl.BlockSpec(memory_space=pl.ANY)


def params(mib):
    return pltpu.CompilerParams(vmem_limit_bytes=mib * 2**20)


def exchange(x, axis):
    return lax.all_to_all(x, axis, 0, 0, tiled=True)


def repeat(x, n):
    return jnp.broadcast_to(x[None], (n,) + x.shape)


def tile_sum(x):
    return jnp.sum(x.astype(F32), axis=0).astype(BF)


def add_up(*terms):
    total = terms[0].astype(F32)
    for term in terms[1:]:
        total = total + term.astype(F32)
    return total.astype(BF)


def swap_cores(x):
    return lax.ppermute(x, "core", [(0, 1), (1, 0)])


def mirrored_shift(x, by):
    pairs = []
    for y in range(Y):
        pairs.append((y * CORE, (y + by) % Y * CORE))
        pairs.append((y * CORE + 1, (y - by) % Y * CORE + 1))
    return lax.ppermute(x, ("yh", "yl", "core"), pairs)


def neighbour_exchange(x):
    pairs = []
    for y in range(Y):
        up = 1 if y % 2 == 0 else -1
        pairs.append((y * CORE, (y + up) % Y * CORE))
        pairs.append((y * CORE + 1, (y - up) % Y * CORE + 1))
    return lax.ppermute(x, ("yh", "yl", "core"), pairs)


def per_device(features, adj_tiles, tile_rows, tile_cols, tile_count, weight, cotangent):
    adj = adj_tiles[0, 0]
    rows = tile_rows[0, 0]
    cols = tile_cols[0, 0]
    count = tile_count[0]
    core = lax.axis_index("core")
    y = lax.axis_index(("yh", "yl"))

    row_core = rows % CORE
    row_zh = rows // CORE % ZH
    row_y = rows // (CORE * ZH)
    row_ahead = (row_y - y) % Y
    foreign = (row_core != core).astype(jnp.int32)
    steps = jnp.where(row_core == 0, row_ahead, (Y - row_ahead) % Y)
    sent_place = foreign * HALF + steps * ZH + row_zh
    gather_place = foreign * HALF + (row_ahead % 2) * QUARTER + row_y // YL * ZH + row_zh

    panels = exchange(repeat(features[0], ZL), "zl")
    panels = exchange(repeat(panels, X), "x").reshape(COLS, TILE, F)
    tiles = cotangent.reshape(HALF * CORE, TILE, F)
    first_own = y * (ZH * CORE) + core
    own_grads = pl.pallas_call(
        pick_kernel,
        out_shape=jax.ShapeDtypeStruct((ZH, TILE, F), BF),
        in_specs=[SMEM, HBM],
        out_specs=VMEM,
        scratch_shapes=[pltpu.SemaphoreType.DMA((ZH,))],
        compiler_params=params(4),
    )(first_own[None], tiles)
    panels, own_grads = lax.optimization_barrier((panels, own_grads))
    mine, theirs = pl.pallas_call(
        forward_kernel,
        out_shape=[
            jax.ShapeDtypeStruct((HALF, TILE, F), BF),
            jax.ShapeDtypeStruct((HALF, TILE, F), BF),
        ],
        in_specs=[SMEM, SMEM, SMEM, VMEM, VMEM],
        out_specs=[VMEM, VMEM],
        scratch_shapes=[pltpu.VMEM((CORE * HALF, TILE, F), F32)],
        compiler_params=params(18),
    )(sent_place, cols, count, adj, panels)
    chip = add_up(mine, swap_cores(theirs)).reshape(Y, ZH, TILE, F)
    from_four = mirrored_shift(chip[4], 2)
    from_three = mirrored_shift(chip[3], 1)
    from_minus_three = mirrored_shift(chip[5], -1)
    ones = [mirrored_shift(chip[1], 1), mirrored_shift(chip[7], -1)]
    minus_two = mirrored_shift(add_up(chip[6], from_minus_three), -2)
    plus_two = mirrored_shift(add_up(chip[2], from_four, from_three), 2)
    y_sum = add_up(chip[0], *ones, minus_two, plus_two)
    parts = lax.all_gather(y_sum, "zh", axis=0)

    layer_out, here = pl.pallas_call(
        middle_kernel,
        out_shape=[
            jax.ShapeDtypeStruct((TILE, F), BF),
            jax.ShapeDtypeStruct((ZH, TILE, F), BF),
        ],
        in_specs=[SMEM, VMEM, VMEM, VMEM],
        out_specs=[VMEM, VMEM],
        scratch_shapes=[pltpu.VMEM((ZH, TILE, F), F32)],
        compiler_params=params(8),
    )(lax.axis_index("zh")[None], parts, weight, own_grads)

    near = lax.all_gather(here, "yh", axis=0).reshape(QUARTER, TILE, F)
    far = neighbour_exchange(near)
    other_near, other_far = swap_cores(near), swap_cores(far)
    column_part = pl.pallas_call(
        backward_kernel,
        out_shape=jax.ShapeDtypeStruct((COLS, TILE, F), BF),
        in_specs=[SMEM] * 3 + [VMEM] * 5,
        out_specs=VMEM,
        scratch_shapes=[pltpu.VMEM((COLS, TILE, F), F32)],
        compiler_params=params(14),
    )(cols, gather_place, count, adj, near, far, other_near, other_far)
    x_sum = tile_sum(exchange(column_part.reshape(X, ZL, TILE, F), "x"))
    grad_input = tile_sum(exchange(x_sum, "zl"))
    return (layer_out, grad_input[None])


def solution(mesh):
    fine = Mesh(
        mesh.devices.reshape(X, ZL, YH, YL, ZH, CORE), ("x", "zl", "yh", "yl", "zh", "core")
    )
    row, sect = ("x", "zl"), ("yh", "yl", "zh", "core")
    in_specs = (
        P(row, sect, None),
        P(row, sect, None, None, None),
        P(row, sect, None),
        P(row, sect, None),
        P(row, sect),
        P(),
        P(row, None),
    )
    out_specs = (P(row + sect, None), P(row, sect, None))
    return jax.shard_map(
        per_device, mesh=fine, in_specs=in_specs, out_specs=out_specs, check_vma=False
    )
```

```python
import jax
import jax.numpy as jnp
from jax import lax
from jax.experimental import pallas as pl
from jax.experimental.pallas import tpu as pltpu
from jax.sharding import Mesh
from jax.sharding import PartitionSpec as P

TILE = 128
F = 256
X, ZL, YH, YL, ZH, CORE = 4, 4, 4, 2, 3, 2
Y = YH * YL
COLS = X * ZL
HALF = Y * ZH
QUARTER = YH * ZH
BF = jnp.bfloat16
F32 = jnp.float32
UNROLL = 4
SLOTS = 32


def pick_kernel(own_ref, cotangent_hbm, grads_ref, sems):
    copies = []
    for k in range(ZH):
        copies.append(
            pltpu.make_async_copy(
                cotangent_hbm.at[own_ref[0] + k * CORE], grads_ref.at[k], sems.at[k]
            )
        )
    for copy in copies:
        copy.start()
    for copy in copies:
        copy.wait()


def repeat_kernel(x_ref, out_ref):
    for k in range(X):
        out_ref[k] = x_ref[...]


def forward_kernel(
    plan_ref, adj_ref, panels_ref, mine_ref, theirs_ref, acc_ref
):
    acc_ref[...] = jnp.zeros_like(acc_ref)

    def step(i, carry):
        products = []
        for k in range(UNROLL):
            t = i * UNROLL + k
            products.append(
                jnp.dot(adj_ref[t], panels_ref[plan_ref[2 * t + 1]], preferred_element_type=F32)
            )
        for k in range(UNROLL):
            acc_ref[plan_ref[2 * (i * UNROLL + k)]] += products[k]
        return carry

    lax.fori_loop(0, plan_ref[2 * SLOTS] // UNROLL, step, 0)
    theirs_ref[...] = acc_ref[HALF:].astype(BF)
    mine_ref[...] = acc_ref[:HALF].astype(BF)

def chip_kernel(mine_ref, other_ref, *out_refs):
    for k, out_ref in enumerate(out_refs):
        at = slice(k * ZH, (k + 1) * ZH)
        out_ref[...] = (mine_ref[at].astype(F32) + other_ref[at].astype(F32)).astype(BF)


def backward_kernel(
    plan_ref, adj_ref, near_ref, far_ref, other_near_ref, other_far_ref, out_ref, acc_ref
):
    acc_ref[...] = jnp.zeros_like(acc_ref)

    def step(i, carry):
        products = []
        for k in range(UNROLL):
            t = i * UNROLL + k
            src = plan_ref[2 * t + 1]
            group = src // QUARTER
            place = src - group * QUARTER
            near = jnp.where(group < 2, near_ref[place], other_near_ref[place])
            far = jnp.where(group < 2, far_ref[place], other_far_ref[place])
            grad = jnp.where(lax.rem(group, 2) == 0, near, far)
            products.append(
                lax.dot_general(
                    adj_ref[t], grad, (((0,), (0,)), ((), ())), preferred_element_type=F32
                )
            )
        for k in range(UNROLL):
            acc_ref[plan_ref[2 * (i * UNROLL + k)]] += products[k]
        return carry

    lax.fori_loop(0, plan_ref[2 * SLOTS] // UNROLL, step, 0)
    out_ref[...] = acc_ref[...].astype(BF)


def middle_kernel(zh_ref, parts_ref, weight_ref, cotangent_ref, layer_ref, grad_ref, out_ref):
    summed = parts_ref[0].astype(F32)
    for k in range(1, ZH):
        summed = summed + parts_ref[k].astype(F32)
    summed = summed.reshape(ZH * TILE, F)
    weight = weight_ref[...]
    pre_act = jnp.dot(summed.astype(BF), weight, preferred_element_type=F32)
    sigma = jax.nn.sigmoid(pre_act)
    out_ref[...] = (pre_act * sigma).reshape(ZH, TILE, F)
    layer_ref[...] = out_ref[zh_ref[0]].astype(BF)
    cotangent = cotangent_ref[...].reshape(ZH * TILE, F).astype(F32)
    grad_pre = (cotangent * sigma * (1.0 + pre_act * (1.0 - sigma))).astype(BF)
    grad = lax.dot_general(
        grad_pre, weight, (((1,), (1,)), ((), ())), preferred_element_type=F32
    ).astype(BF)
    grad_ref[...] = grad.reshape(ZH, TILE, F)


SMEM = pl.BlockSpec(memory_space=pltpu.SMEM)
VMEM = pl.BlockSpec(memory_space=pltpu.VMEM)
HBM = pl.BlockSpec(memory_space=pl.ANY)


def params(mib):
    return pltpu.CompilerParams(vmem_limit_bytes=mib * 2**20)


def exchange(x, axis):
    return lax.all_to_all(x, axis, 0, 0, tiled=True)


def repeat(x, n):
    return jnp.broadcast_to(x[None], (n,) + x.shape)


def tile_sum(x):
    return jnp.sum(x.astype(F32), axis=0).astype(BF)


def add_up(*terms):
    total = terms[0].astype(F32)
    for term in terms[1:]:
        total = total + term.astype(F32)
    return total.astype(BF)


def swap_cores(x):
    return lax.ppermute(x, "core", [(0, 1), (1, 0)])


def mirrored_shift(x, by):
    pairs = []
    for y in range(Y):
        pairs.append((y * CORE, (y + by) % Y * CORE))
        pairs.append((y * CORE + 1, (y - by) % Y * CORE + 1))
    return lax.ppermute(x, ("yh", "yl", "core"), pairs)


def neighbour_exchange(x):
    pairs = []
    for y in range(Y):
        up = 1 if y % 2 == 0 else -1
        pairs.append((y * CORE, (y + up) % Y * CORE))
        pairs.append((y * CORE + 1, (y - up) % Y * CORE + 1))
    return lax.ppermute(x, ("yh", "yl", "core"), pairs)


def slot_plan(targets, sources, count):
    return jnp.concatenate([jnp.stack([targets, sources], axis=1).reshape(2 * SLOTS), count])


def per_device(features, adj_tiles, tile_rows, tile_cols, tile_count, weight, cotangent):
    adj = adj_tiles[0, 0]
    rows = tile_rows[0, 0]
    cols = tile_cols[0, 0]
    count = tile_count[0]
    core = lax.axis_index("core")
    y = lax.axis_index(("yh", "yl"))

    row_core = rows % CORE
    row_zh = rows // CORE % ZH
    row_y = rows // (CORE * ZH)
    row_ahead = (row_y - y) % Y
    foreign = (row_core != core).astype(jnp.int32)
    steps = jnp.where(row_core == 0, row_ahead, (Y - row_ahead) % Y)
    sent_place = foreign * HALF + steps * ZH + row_zh
    gather_place = foreign * HALF + (row_ahead % 2) * QUARTER + row_y // YL * ZH + row_zh

    forward_plan = slot_plan(sent_place, cols, count)
    backward_plan = slot_plan(cols, gather_place, count)

    panels = lax.all_gather(features[0], "zl", axis=0)
    copies = pl.pallas_call(
        repeat_kernel,
        out_shape=jax.ShapeDtypeStruct((X, ZL, TILE, F), BF),
        in_specs=[VMEM],
        out_specs=VMEM,
        compiler_params=params(6),
    )(panels)
    panels = exchange(copies, "x").reshape(COLS, TILE, F)
    tiles = cotangent.reshape(HALF * CORE, TILE, F)
    first_own = y * (ZH * CORE) + core
    own_grads = pl.pallas_call(
        pick_kernel,
        out_shape=jax.ShapeDtypeStruct((ZH, TILE, F), BF),
        in_specs=[SMEM, HBM],
        out_specs=VMEM,
        scratch_shapes=[pltpu.SemaphoreType.DMA((ZH,))],
        compiler_params=params(4),
    )(first_own[None], tiles)
    panels, own_grads, forward_plan, backward_plan = lax.optimization_barrier(
        (panels, own_grads, forward_plan, backward_plan)
    )
    mine, theirs = pl.pallas_call(
        forward_kernel,
        out_shape=[
            jax.ShapeDtypeStruct((HALF, TILE, F), BF),
            jax.ShapeDtypeStruct((HALF, TILE, F), BF),
        ],
        in_specs=[SMEM, VMEM, VMEM],
        out_specs=[VMEM, VMEM],
        scratch_shapes=[pltpu.VMEM((CORE * HALF, TILE, F), F32)],
        compiler_params=params(18),
    )(forward_plan, adj, panels)
    chip = pl.pallas_call(
        chip_kernel,
        out_shape=[jax.ShapeDtypeStruct((ZH, TILE, F), BF)] * Y,
        compiler_params=params(8),
    )(mine, swap_cores(theirs))
    from_four = mirrored_shift(chip[4], 2)
    from_three = mirrored_shift(chip[3], 1)
    from_minus_three = mirrored_shift(chip[5], -1)
    ones = [mirrored_shift(chip[1], 1), mirrored_shift(chip[7], -1)]
    minus_two = mirrored_shift(add_up(chip[6], from_minus_three), -2)
    plus_two = mirrored_shift(add_up(chip[2], from_four, from_three), 2)
    y_sum = add_up(chip[0], *ones, minus_two, plus_two)
    parts = lax.all_gather(y_sum, "zh", axis=0)

    layer_out, here = pl.pallas_call(
        middle_kernel,
        out_shape=[
            jax.ShapeDtypeStruct((TILE, F), BF),
            jax.ShapeDtypeStruct((ZH, TILE, F), BF),
        ],
        in_specs=[SMEM, VMEM, VMEM, VMEM],
        out_specs=[VMEM, VMEM],
        scratch_shapes=[pltpu.VMEM((ZH, TILE, F), F32)],
        compiler_params=params(8),
    )(lax.axis_index("zh")[None], parts, weight, own_grads)

    near = lax.all_gather(here, "yh", axis=0).reshape(QUARTER, TILE, F)
    far = neighbour_exchange(near)
    other_near, other_far = swap_cores(near), swap_cores(far)
    column_part = pl.pallas_call(
        backward_kernel,
        out_shape=jax.ShapeDtypeStruct((COLS, TILE, F), BF),
        in_specs=[SMEM] + [VMEM] * 5,
        out_specs=VMEM,
        scratch_shapes=[pltpu.VMEM((COLS, TILE, F), F32)],
        compiler_params=params(14),
    )(backward_plan, adj, near, far, other_near, other_far)
    x_sum = tile_sum(exchange(column_part.reshape(X, ZL, TILE, F), "x"))
    grad_input = tile_sum(exchange(x_sum, "zl"))
    return (layer_out, grad_input[None])


def solution(mesh):
    fine = Mesh(
        mesh.devices.reshape(X, ZL, YH, YL, ZH, CORE), ("x", "zl", "yh", "yl", "zh", "core")
    )
    row, sect = ("x", "zl"), ("yh", "yl", "zh", "core")
    in_specs = (
        P(row, sect, None),
        P(row, sect, None, None, None),
        P(row, sect, None),
        P(row, sect, None),
        P(row, sect),
        P(),
        P(row, None),
    )
    out_specs = (P(row + sect, None), P(row, sect, None))
    return jax.shard_map(
        per_device, mesh=fine, in_specs=in_specs, out_specs=out_specs, check_vma=False
    )
```

```python
import jax
import jax.numpy as jnp
from jax import lax
from jax.experimental import pallas as pl
from jax.experimental.pallas import tpu as pltpu
from jax.sharding import Mesh
from jax.sharding import PartitionSpec as P

TILE = 128
F = 256
X, ZL, YH, YL, ZH, CORE = 4, 4, 4, 2, 3, 2
Y = YH * YL
COLS = X * ZL
HALF = Y * ZH
QUARTER = YH * ZH
BF = jnp.bfloat16
F32 = jnp.float32
UNROLL = 4
SENT_STEPS = (3, 4, 5, 0, 1, 2, 6, 7)
EARLY = 3
SLOTS = 32


def pick_kernel(own_ref, cotangent_hbm, grads_ref, sems):
    copies = []
    for k in range(ZH):
        copies.append(
            pltpu.make_async_copy(
                cotangent_hbm.at[own_ref[0] + k * CORE], grads_ref.at[k], sems.at[k]
            )
        )
    for copy in copies:
        copy.start()
    for copy in copies:
        copy.wait()


def repeat_kernel(x_ref, out_ref):
    for k in range(X):
        out_ref[k] = x_ref[...]


def forward_kernel(
    plan_ref, adj_ref, panels_ref, early_mine_ref, mine_ref, early_theirs_ref, theirs_ref, acc_ref
):
    acc_ref[...] = jnp.zeros_like(acc_ref)

    def step(i, carry):
        products = []
        for k in range(UNROLL):
            t = i * UNROLL + k
            products.append(
                jnp.dot(adj_ref[t], panels_ref[plan_ref[2 * t + 1]], preferred_element_type=F32)
            )
        for k in range(UNROLL):
            acc_ref[plan_ref[2 * (i * UNROLL + k)]] += products[k]
        return carry

    lax.fori_loop(0, plan_ref[2 * SLOTS] // UNROLL, step, 0)
    split = EARLY * ZH
    early_theirs_ref[...] = acc_ref[HALF : HALF + split].astype(BF)
    theirs_ref[...] = acc_ref[HALF + split :].astype(BF)
    early_mine_ref[...] = acc_ref[:split].astype(BF)
    mine_ref[...] = acc_ref[split:HALF].astype(BF)

def chip_kernel(mine_ref, other_ref, *out_refs):
    for k, out_ref in enumerate(out_refs):
        at = slice(k * ZH, (k + 1) * ZH)
        out_ref[...] = (mine_ref[at].astype(F32) + other_ref[at].astype(F32)).astype(BF)


def backward_kernel(
    plan_ref, adj_ref, near_ref, far_ref, other_near_ref, other_far_ref, out_ref, acc_ref
):
    acc_ref[...] = jnp.zeros_like(acc_ref)

    def step(i, carry):
        products = []
        for k in range(UNROLL):
            t = i * UNROLL + k
            src = plan_ref[2 * t + 1]
            group = src // QUARTER
            place = src - group * QUARTER
            near = jnp.where(group < 2, near_ref[place], other_near_ref[place])
            far = jnp.where(group < 2, far_ref[place], other_far_ref[place])
            grad = jnp.where(lax.rem(group, 2) == 0, near, far)
            products.append(
                lax.dot_general(
                    adj_ref[t], grad, (((0,), (0,)), ((), ())), preferred_element_type=F32
                )
            )
        for k in range(UNROLL):
            acc_ref[plan_ref[2 * (i * UNROLL + k)]] += products[k]
        return carry

    lax.fori_loop(0, plan_ref[2 * SLOTS] // UNROLL, step, 0)
    out_ref[...] = acc_ref[...].astype(BF)


def middle_kernel(zh_ref, parts_ref, weight_ref, cotangent_ref, layer_ref, grad_ref, out_ref):
    summed = parts_ref[0].astype(F32)
    for k in range(1, ZH):
        summed = summed + parts_ref[k].astype(F32)
    summed = summed.reshape(ZH * TILE, F)
    weight = weight_ref[...]
    pre_act = jnp.dot(summed.astype(BF), weight, preferred_element_type=F32)
    sigma = jax.nn.sigmoid(pre_act)
    out_ref[...] = (pre_act * sigma).reshape(ZH, TILE, F)
    layer_ref[...] = out_ref[zh_ref[0]].astype(BF)
    cotangent = cotangent_ref[...].reshape(ZH * TILE, F).astype(F32)
    grad_pre = (cotangent * sigma * (1.0 + pre_act * (1.0 - sigma))).astype(BF)
    grad = lax.dot_general(
        grad_pre, weight, (((1,), (1,)), ((), ())), preferred_element_type=F32
    ).astype(BF)
    grad_ref[...] = grad.reshape(ZH, TILE, F)


SMEM = pl.BlockSpec(memory_space=pltpu.SMEM)
VMEM = pl.BlockSpec(memory_space=pltpu.VMEM)
HBM = pl.BlockSpec(memory_space=pl.ANY)


def params(mib):
    return pltpu.CompilerParams(vmem_limit_bytes=mib * 2**20)


def exchange(x, axis):
    return lax.all_to_all(x, axis, 0, 0, tiled=True)


def repeat(x, n):
    return jnp.broadcast_to(x[None], (n,) + x.shape)


def tile_sum(x):
    return jnp.sum(x.astype(F32), axis=0).astype(BF)


def add_up(*terms):
    total = terms[0].astype(F32)
    for term in terms[1:]:
        total = total + term.astype(F32)
    return total.astype(BF)


def swap_cores(x):
    return lax.ppermute(x, "core", [(0, 1), (1, 0)])


def mirrored_shift(x, by):
    pairs = []
    for y in range(Y):
        pairs.append((y * CORE, (y + by) % Y * CORE))
        pairs.append((y * CORE + 1, (y - by) % Y * CORE + 1))
    return lax.ppermute(x, ("yh", "yl", "core"), pairs)


def neighbour_exchange(x):
    pairs = []
    for y in range(Y):
        up = 1 if y % 2 == 0 else -1
        pairs.append((y * CORE, (y + up) % Y * CORE))
        pairs.append((y * CORE + 1, (y - up) % Y * CORE + 1))
    return lax.ppermute(x, ("yh", "yl", "core"), pairs)


def slot_plan(targets, sources, count):
    return jnp.concatenate([jnp.stack([targets, sources], axis=1).reshape(2 * SLOTS), count])


def per_device(features, adj_tiles, tile_rows, tile_cols, tile_count, weight, cotangent):
    adj = adj_tiles[0, 0]
    rows = tile_rows[0, 0]
    cols = tile_cols[0, 0]
    count = tile_count[0]
    core = lax.axis_index("core")
    y = lax.axis_index(("yh", "yl"))

    row_core = rows % CORE
    row_zh = rows // CORE % ZH
    row_y = rows // (CORE * ZH)
    row_ahead = (row_y - y) % Y
    foreign = (row_core != core).astype(jnp.int32)
    steps = jnp.where(row_core == 0, row_ahead, (Y - row_ahead) % Y)
    step_place = jnp.zeros_like(rows)
    for place, k in enumerate(SENT_STEPS):
        step_place = jnp.where(steps == k, place, step_place)
    sent_place = foreign * HALF + step_place * ZH + row_zh
    gather_place = foreign * HALF + (row_ahead % 2) * QUARTER + row_y // YL * ZH + row_zh

    forward_plan = slot_plan(sent_place, cols, count)
    backward_plan = slot_plan(cols, gather_place, count)

    panels = lax.all_gather(features[0], "zl", axis=0)
    copies = pl.pallas_call(
        repeat_kernel,
        out_shape=jax.ShapeDtypeStruct((X, ZL, TILE, F), BF),
        in_specs=[VMEM],
        out_specs=VMEM,
        compiler_params=params(6),
    )(panels)
    panels = exchange(copies, "x").reshape(COLS, TILE, F)
    tiles = cotangent.reshape(HALF * CORE, TILE, F)
    first_own = y * (ZH * CORE) + core
    own_grads = pl.pallas_call(
        pick_kernel,
        out_shape=jax.ShapeDtypeStruct((ZH, TILE, F), BF),
        in_specs=[SMEM, HBM],
        out_specs=VMEM,
        scratch_shapes=[pltpu.SemaphoreType.DMA((ZH,))],
        compiler_params=params(4),
    )(first_own[None], tiles)
    panels, own_grads, forward_plan, backward_plan = lax.optimization_barrier(
        (panels, own_grads, forward_plan, backward_plan)
    )
    early_mine, mine, early_theirs, theirs = pl.pallas_call(
        forward_kernel,
        out_shape=[
            jax.ShapeDtypeStruct((EARLY * ZH, TILE, F), BF),
            jax.ShapeDtypeStruct(((Y - EARLY) * ZH, TILE, F), BF),
        ]
        * CORE,
        in_specs=[SMEM, VMEM, VMEM],
        out_specs=[VMEM] * 4,
        scratch_shapes=[pltpu.VMEM((CORE * HALF, TILE, F), F32)],
        compiler_params=params(18),
    )(forward_plan, adj, panels)
    chip = {}
    for steps_here, here_part, there_part in (
        (SENT_STEPS[:EARLY], early_mine, early_theirs),
        (SENT_STEPS[EARLY:], mine, theirs),
    ):
        sums = pl.pallas_call(
            chip_kernel,
            out_shape=[jax.ShapeDtypeStruct((ZH, TILE, F), BF)] * len(steps_here),
            compiler_params=params(8),
        )(here_part, swap_cores(there_part))
        chip.update(zip(steps_here, sums))
    from_four = mirrored_shift(chip[4], 2)
    from_three = mirrored_shift(chip[3], 1)
    from_minus_three = mirrored_shift(chip[5], -1)
    ones = [mirrored_shift(chip[1], 1), mirrored_shift(chip[7], -1)]
    minus_two = mirrored_shift(add_up(chip[6], from_minus_three), -2)
    plus_two = mirrored_shift(add_up(chip[2], from_four, from_three), 2)
    y_sum = add_up(chip[0], *ones, minus_two, plus_two)
    parts = lax.all_gather(y_sum, "zh", axis=0)

    layer_out, here = pl.pallas_call(
        middle_kernel,
        out_shape=[
            jax.ShapeDtypeStruct((TILE, F), BF),
            jax.ShapeDtypeStruct((ZH, TILE, F), BF),
        ],
        in_specs=[SMEM, VMEM, VMEM, VMEM],
        out_specs=[VMEM, VMEM],
        scratch_shapes=[pltpu.VMEM((ZH, TILE, F), F32)],
        compiler_params=params(8),
    )(lax.axis_index("zh")[None], parts, weight, own_grads)

    near = lax.all_gather(here, "yh", axis=0).reshape(QUARTER, TILE, F)
    far = neighbour_exchange(near)
    other_near, other_far = swap_cores(near), swap_cores(far)
    column_part = pl.pallas_call(
        backward_kernel,
        out_shape=jax.ShapeDtypeStruct((COLS, TILE, F), BF),
        in_specs=[SMEM] + [VMEM] * 5,
        out_specs=VMEM,
        scratch_shapes=[pltpu.VMEM((COLS, TILE, F), F32)],
        compiler_params=params(14),
    )(backward_plan, adj, near, far, other_near, other_far)
    x_sum = tile_sum(exchange(column_part.reshape(X, ZL, TILE, F), "x"))
    grad_input = tile_sum(exchange(x_sum, "zl"))
    return (layer_out, grad_input[None])


def solution(mesh):
    fine = Mesh(
        mesh.devices.reshape(X, ZL, YH, YL, ZH, CORE), ("x", "zl", "yh", "yl", "zh", "core")
    )
    row, sect = ("x", "zl"), ("yh", "yl", "zh", "core")
    in_specs = (
        P(row, sect, None),
        P(row, sect, None, None, None),
        P(row, sect, None),
        P(row, sect, None),
        P(row, sect),
        P(),
        P(row, None),
    )
    out_specs = (P(row + sect, None), P(row, sect, None))
    return jax.shard_map(
        per_device, mesh=fine, in_specs=in_specs, out_specs=out_specs, check_vma=False
    )
```

```python
import jax
import jax.numpy as jnp
from jax import lax
from jax.experimental import pallas as pl
from jax.experimental.pallas import tpu as pltpu
from jax.sharding import Mesh
from jax.sharding import PartitionSpec as P

TILE = 128
F = 256
X, ZL, YH, YL, ZH, CORE = 4, 4, 4, 2, 3, 2
Y = YH * YL
COLS = X * ZL
HALF = Y * ZH
QUARTER = YH * ZH
BF = jnp.bfloat16
F32 = jnp.float32
UNROLL = 4
SLOTS = 32


def pick_kernel(own_ref, cotangent_hbm, grads_ref, sems):
    copies = []
    for k in range(ZH):
        copies.append(
            pltpu.make_async_copy(
                cotangent_hbm.at[own_ref[0] + k * CORE], grads_ref.at[k], sems.at[k]
            )
        )
    for copy in copies:
        copy.start()
    for copy in copies:
        copy.wait()


def repeat_kernel(x_ref, out_ref):
    for k in range(X):
        out_ref[k] = x_ref[...]


def forward_kernel(
    plan_ref, adj_ref, panels_ref, mine_ref, theirs_ref, acc_ref
):
    acc_ref[...] = jnp.zeros_like(acc_ref)

    def step(i, carry):
        products = []
        for k in range(UNROLL):
            t = i * UNROLL + k
            products.append(
                jnp.dot(adj_ref[t], panels_ref[plan_ref[2 * t + 1]], preferred_element_type=F32)
            )
        for k in range(UNROLL):
            acc_ref[plan_ref[2 * (i * UNROLL + k)]] += products[k]
        return carry

    lax.fori_loop(0, plan_ref[2 * SLOTS] // UNROLL, step, 0)
    theirs_ref[...] = acc_ref[HALF:].astype(BF)
    mine_ref[...] = acc_ref[:HALF].astype(BF)

def chip_kernel(mine_ref, other_ref, ahead_ref, *out_refs):
    targets = [ahead_ref.at[:ZH], ahead_ref.at[ZH:], *out_refs]
    for k, target in zip((1, 3, 0, 2, 4, 5, 6, 7), targets):
        at = slice(k * ZH, (k + 1) * ZH)
        target[...] = (mine_ref[at].astype(F32) + other_ref[at].astype(F32)).astype(BF)


def backward_kernel(
    plan_ref, adj_ref, near_ref, far_ref, other_near_ref, other_far_ref, out_ref, acc_ref
):
    acc_ref[...] = jnp.zeros_like(acc_ref)

    def step(i, carry):
        products = []
        for k in range(UNROLL):
            t = i * UNROLL + k
            src = plan_ref[2 * t + 1]
            group = src // QUARTER
            place = src - group * QUARTER
            near = jnp.where(group < 2, near_ref[place], other_near_ref[place])
            far = jnp.where(group < 2, far_ref[place], other_far_ref[place])
            grad = jnp.where(lax.rem(group, 2) == 0, near, far)
            products.append(
                lax.dot_general(
                    adj_ref[t], grad, (((0,), (0,)), ((), ())), preferred_element_type=F32
                )
            )
        for k in range(UNROLL):
            acc_ref[plan_ref[2 * (i * UNROLL + k)]] += products[k]
        return carry

    lax.fori_loop(0, plan_ref[2 * SLOTS] // UNROLL, step, 0)
    out_ref[...] = acc_ref[...].astype(BF)


def middle_kernel(zh_ref, parts_ref, weight_ref, cotangent_ref, layer_ref, grad_ref, out_ref):
    summed = parts_ref[0].astype(F32)
    for k in range(1, ZH):
        summed = summed + parts_ref[k].astype(F32)
    summed = summed.reshape(ZH * TILE, F)
    weight = weight_ref[...]
    pre_act = jnp.dot(summed.astype(BF), weight, preferred_element_type=F32)
    sigma = jax.nn.sigmoid(pre_act)
    out_ref[...] = (pre_act * sigma).reshape(ZH, TILE, F)
    layer_ref[...] = out_ref[zh_ref[0]].astype(BF)
    cotangent = cotangent_ref[...].reshape(ZH * TILE, F).astype(F32)
    grad_pre = (cotangent * sigma * (1.0 + pre_act * (1.0 - sigma))).astype(BF)
    grad = lax.dot_general(
        grad_pre, weight, (((1,), (1,)), ((), ())), preferred_element_type=F32
    ).astype(BF)
    grad_ref[...] = grad.reshape(ZH, TILE, F)


SMEM = pl.BlockSpec(memory_space=pltpu.SMEM)
VMEM = pl.BlockSpec(memory_space=pltpu.VMEM)
HBM = pl.BlockSpec(memory_space=pl.ANY)


def params(mib):
    return pltpu.CompilerParams(vmem_limit_bytes=mib * 2**20)


def exchange(x, axis):
    return lax.all_to_all(x, axis, 0, 0, tiled=True)


def repeat(x, n):
    return jnp.broadcast_to(x[None], (n,) + x.shape)


def tile_sum(x):
    return jnp.sum(x.astype(F32), axis=0).astype(BF)


def add_up(*terms):
    total = terms[0].astype(F32)
    for term in terms[1:]:
        total = total + term.astype(F32)
    return total.astype(BF)


def swap_cores(x):
    return lax.ppermute(x, "core", [(0, 1), (1, 0)])


def mirrored_shift(x, by):
    pairs = []
    for y in range(Y):
        pairs.append((y * CORE, (y + by) % Y * CORE))
        pairs.append((y * CORE + 1, (y - by) % Y * CORE + 1))
    return lax.ppermute(x, ("yh", "yl", "core"), pairs)


def neighbour_exchange(x):
    pairs = []
    for y in range(Y):
        up = 1 if y % 2 == 0 else -1
        pairs.append((y * CORE, (y + up) % Y * CORE))
        pairs.append((y * CORE + 1, (y - up) % Y * CORE + 1))
    return lax.ppermute(x, ("yh", "yl", "core"), pairs)


def slot_plan(targets, sources, count):
    return jnp.concatenate([jnp.stack([targets, sources], axis=1).reshape(2 * SLOTS), count])


def per_device(features, adj_tiles, tile_rows, tile_cols, tile_count, weight, cotangent):
    adj = adj_tiles[0, 0]
    rows = tile_rows[0, 0]
    cols = tile_cols[0, 0]
    count = tile_count[0]
    core = lax.axis_index("core")
    y = lax.axis_index(("yh", "yl"))

    row_core = rows % CORE
    row_zh = rows // CORE % ZH
    row_y = rows // (CORE * ZH)
    row_ahead = (row_y - y) % Y
    foreign = (row_core != core).astype(jnp.int32)
    steps = jnp.where(row_core == 0, row_ahead, (Y - row_ahead) % Y)
    sent_place = foreign * HALF + steps * ZH + row_zh
    gather_place = foreign * HALF + (row_ahead % 2) * QUARTER + row_y // YL * ZH + row_zh

    forward_plan = slot_plan(sent_place, cols, count)
    backward_plan = slot_plan(cols, gather_place, count)

    panels = lax.all_gather(features[0], "zl", axis=0)
    copies = pl.pallas_call(
        repeat_kernel,
        out_shape=jax.ShapeDtypeStruct((X, ZL, TILE, F), BF),
        in_specs=[VMEM],
        out_specs=VMEM,
        compiler_params=params(6),
    )(panels)
    panels = exchange(copies, "x").reshape(COLS, TILE, F)
    tiles = cotangent.reshape(HALF * CORE, TILE, F)
    first_own = y * (ZH * CORE) + core
    own_grads = pl.pallas_call(
        pick_kernel,
        out_shape=jax.ShapeDtypeStruct((ZH, TILE, F), BF),
        in_specs=[SMEM, HBM],
        out_specs=VMEM,
        scratch_shapes=[pltpu.SemaphoreType.DMA((ZH,))],
        compiler_params=params(4),
    )(first_own[None], tiles)
    panels, own_grads, forward_plan, backward_plan = lax.optimization_barrier(
        (panels, own_grads, forward_plan, backward_plan)
    )
    mine, theirs = pl.pallas_call(
        forward_kernel,
        out_shape=[
            jax.ShapeDtypeStruct((HALF, TILE, F), BF),
            jax.ShapeDtypeStruct((HALF, TILE, F), BF),
        ],
        in_specs=[SMEM, VMEM, VMEM],
        out_specs=[VMEM, VMEM],
        scratch_shapes=[pltpu.VMEM((CORE * HALF, TILE, F), F32)],
        compiler_params=params(18),
    )(forward_plan, adj, panels)
    to_next, *sums = pl.pallas_call(
        chip_kernel,
        out_shape=[
            jax.ShapeDtypeStruct((2 * ZH, TILE, F), BF),
            *[jax.ShapeDtypeStruct((ZH, TILE, F), BF)] * (Y - 2),
        ],
        compiler_params=params(8),
    )(mine, swap_cores(theirs))
    chip = dict(zip((0, 2, 4, 5, 6, 7), sums))
    from_four = mirrored_shift(chip[4], 2)
    from_behind = mirrored_shift(to_next, 1)
    from_one, from_three = from_behind[:ZH], from_behind[ZH:]
    from_minus_three = mirrored_shift(chip[5], -1)
    ones = [from_one, mirrored_shift(chip[7], -1)]
    minus_two = mirrored_shift(add_up(chip[6], from_minus_three), -2)
    plus_two = mirrored_shift(add_up(chip[2], from_four, from_three), 2)
    y_sum = add_up(chip[0], *ones, minus_two, plus_two)
    parts = lax.all_gather(y_sum, "zh", axis=0)

    layer_out, here = pl.pallas_call(
        middle_kernel,
        out_shape=[
            jax.ShapeDtypeStruct((TILE, F), BF),
            jax.ShapeDtypeStruct((ZH, TILE, F), BF),
        ],
        in_specs=[SMEM, VMEM, VMEM, VMEM],
        out_specs=[VMEM, VMEM],
        scratch_shapes=[pltpu.VMEM((ZH, TILE, F), F32)],
        compiler_params=params(8),
    )(lax.axis_index("zh")[None], parts, weight, own_grads)

    near = lax.all_gather(here, "yh", axis=0).reshape(QUARTER, TILE, F)
    far = neighbour_exchange(near)
    other_near, other_far = swap_cores(near), swap_cores(far)
    column_part = pl.pallas_call(
        backward_kernel,
        out_shape=jax.ShapeDtypeStruct((COLS, TILE, F), BF),
        in_specs=[SMEM] + [VMEM] * 5,
        out_specs=VMEM,
        scratch_shapes=[pltpu.VMEM((COLS, TILE, F), F32)],
        compiler_params=params(14),
    )(backward_plan, adj, near, far, other_near, other_far)
    x_sum = tile_sum(exchange(column_part.reshape(X, ZL, TILE, F), "x"))
    grad_input = tile_sum(exchange(x_sum, "zl"))
    return (layer_out, grad_input[None])


def solution(mesh):
    fine = Mesh(
        mesh.devices.reshape(X, ZL, YH, YL, ZH, CORE), ("x", "zl", "yh", "yl", "zh", "core")
    )
    row, sect = ("x", "zl"), ("yh", "yl", "zh", "core")
    in_specs = (
        P(row, sect, None),
        P(row, sect, None, None, None),
        P(row, sect, None),
        P(row, sect, None),
        P(row, sect),
        P(),
        P(row, None),
    )
    out_specs = (P(row + sect, None), P(row, sect, None))
    return jax.shard_map(
        per_device, mesh=fine, in_specs=in_specs, out_specs=out_specs, check_vma=False
    )
```
